32 devices in a mesh: replica: 2 (over x), tok: 16 (over z, y, core), sec: 1.
Axes of the slice: x: 2, y: 2, z: 4, core: 2. Of those that a mesh axis runs over, the one named last changes fastest.
Arguments:
- queries: bfloat16 [4096, 8192], P(('replica', 'tok'), 'sec'), parts along dimension 0, may hold values from -96 to 96
- kv_pool: bfloat16 [64, 64, 512], P(('replica', 'tok')), parts along dimension 0, may hold values from -9 to 9
- block_table: int32 [64], P('replica'), parts along dimension 0, may hold values from 0 to 31, each once
- lengths: int32 [8], P('replica'), parts along dimension 0, may hold values from 1 to 1024, 2048 in all
- tokens_ffn: bfloat16 [2048, 3584], P(('replica', 'tok'), 'sec'), parts along dimension 0, may hold values from -6 to 6
- routes: int32 [2048, 3], P(('replica', 'tok')), parts along dimension 0, may hold values from 0 to 5, all different within a row; in each aligned block of 64 rows (0 to 63, 64 to 127, ...) at most 33 rows name the same one
- route_probs: float32 [2048, 3], P(('replica', 'tok')), parts along dimension 0, may hold values from 0.1 to 1
- w_in: bfloat16 [16, 3, 3584, 2, 320], P('tok', None, 'sec'), may hold values from -0.09375 to 0.09375
- w_out: bfloat16 [16, 3, 320, 3584], P('tok', None, None, 'sec'), may hold values from -0.125 to 0.125
Outputs:
- attention: bfloat16 [4096, 8192], P(('replica', 'tok'), 'sec'), parts along dimension 0
- moe_out: bfloat16 [2048, 3584], P(('replica', 'tok'), 'sec'), parts along dimension 0
The draws below stay inside these ranges and needn't reach their ends.
There are 2 independent parts, one for each index of `replica`. The reference program is written for one: setup_inputs(seed, part) draws one part's arguments, and reference() takes and returns one part's arrays. A program takes and returns all parts, laid end to end along the dimension named above; an argument that names none is the same for every part. Nothing has to cross between parts.
Inputs may be any that keep to these rules, and one draw needn't show every extreme that they name: `routes`: in every aligned block of 64 rows, no expert is named by more than 33 rows, a bound that some block reaches.
All inputs are finite; a program needn't handle non-finite values.
Results may differ from the reference program's by a relative error of at most 0.022.
Values may be sent and summed in bfloat16 or wider, within the bound.
A program may use at most 128 MiB of HBM per device.

```python
import math
import jax
import jax.numpy as jnp
import numpy as np
from jax import lax

PAGE = 64
HEADS = 32
HD = 256
SEQS = 4
M_DEV = 64
D = 3584
TOPK = 3
HE = 2560
GROUP = 8
EXP_GROUP = 3
UNITS = 320
TOKENS = 2048
PAGES = 32
EXPERTS = 6
MTOKENS = 1024
CAP = 33
N_TOK = 16


def draw_kv_pool(key, part):
    key = jax.random.fold_in(key, 3)
    noise = jnp.clip(jax.random.normal(key, (PAGES, PAGE, 2 * HD), jnp.float32), -4.5, 4.5)
    return noise.astype(jnp.bfloat16)


def draw_queries(key, part):
    key = jax.random.fold_in(key, 5)
    base = jnp.clip(jax.random.normal(key, (TOKENS, HEADS * HD), jnp.float32), -4.5, 4.5)
    return base.astype(jnp.bfloat16)


def level_of(rng, dims, shards, smallest, high):
    def one(axis_at, shards_of):
        heights = jax.random.uniform(jax.random.fold_in(jax.random.fold_in(rng, 6), axis_at), (shards_of,), jnp.float32, smallest / len(shards), high / len(shards))
        return jnp.repeat(jnp.exp(heights), dims[axis_at] // shards_of).reshape((-1,) + (1,) * (len(dims) - axis_at - 1))

    gain = one(*shards[0])
    for cut in shards[1:]:
        gain = gain * one(*cut)
    return gain


def profile(amount, total, reach, slope):
    weights = [(1 << 20) // math.isqrt(standing ** slope) + 1 for standing in range(2, amount + 1)]
    spare, holding = total - reach - (amount - 1), [1] * (amount - 1)
    while spare > 0:
        candidates = [i for i in range(amount - 1) if holding[i] < reach]
        mass, remaining = sum([weights[i] for i in candidates]), spare
        for i in candidates:
            more = min(reach - holding[i], max(1, remaining * weights[i] // mass), spare)
            holding[i] = holding[i] + more
            spare = spare - more
    return np.array([reach] + holding)


def uneven_parts(rng, count, total, limit, lean):
    if count == 2:
        one = jax.random.randint(rng, (), max(1, total - limit), min(limit, total - 1) + 1)
        return jnp.stack([one, total - one])
    sizes = jnp.asarray(profile(count, total, limit, lean), jnp.int32)
    couples = (count - 1) // 2
    source_of, sink = sizes[1:1 + 2 * couples:2], sizes[2:2 + 2 * couples:2]
    room = jnp.minimum(source_of - 1, limit - sink)
    shifted = jax.random.randint(jax.random.fold_in(rng, 1), (couples,), 0, 1 << 20) % (room + 1)
    sizes = sizes.at[1:1 + 2 * couples:2].set(source_of - shifted).at[2:2 + 2 * couples:2].set(sink + shifted)
    return sizes[jax.random.permutation(jax.random.fold_in(rng, 2), count)]


def assign_block(own_key, own, number, rows, count, top, limit, lean):
    order = jax.random.permutation(own_key, count)
    crowded, usual = load_shares(count, rows * top, limit, lean, True), load_shares(count, rows * top, limit, lean, False)
    places = jnp.arange(count)

    def named(sizes, turn):
        used = int((sizes > 0).sum())
        fixed = max(1, used // 4)
        passed = fixed + (places - fixed + turn * (used - fixed)) % max(1, count - fixed)
        return jnp.zeros((count,), jnp.int32).at[order[jnp.where(places < fixed, places, passed)]].set(jnp.asarray(sizes, jnp.int32))

    sizes = jnp.where(number % 4 == 0, named(crowded, number // 4), named(usual, number - number // 4 - 1))
    mixed = jax.random.permutation(jax.random.fold_in(own, 3), count)
    source_of, taker = mixed[0:count // 2 * 2:2], mixed[1:count // 2 * 2:2]
    slack = jnp.minimum(sizes[source_of] - 1, limit - sizes[taker]) // 2
    slack = jnp.where((source_of == order[0]) | (taker == order[0]) | (sizes[taker] == 0), 0, jnp.maximum(slack, 0))
    passed = jax.random.randint(jax.random.fold_in(own, 4), (count // 2,), 0, 1 << 20) % (slack + 1)
    sizes = sizes.at[source_of].add(-passed).at[taker].add(passed)
    labels = jnp.searchsorted(jnp.cumsum(sizes), jnp.arange(rows * top), side="right").astype(jnp.int32)
    table = labels.reshape(top, rows).T
    table = table[jax.random.permutation(jax.random.fold_in(own, 1), rows)]
    turn = jax.random.randint(jax.random.fold_in(own, 2), (rows, 1), 0, top)
    return jnp.take_along_axis(table, (jnp.arange(top)[None, :] + turn) % top, axis=1)


def load_shares(amount, total, most, skew, full):
    loads = [(1 << 20) // math.isqrt(standing ** skew) + 1 for standing in range(1, amount + 1)]
    largest = most if full else min(most, max(-(-total // amount), total * loads[0] // sum(loads)))
    least = 1 if total - largest >= amount - 1 else 0
    holding, surplus = [largest] + [least] * (amount - 1), total - largest - least * (amount - 1)
    while surplus > 0:
        candidates = [i for i in range(1, amount) if holding[i] < largest] or [i for i in range(1, amount) if holding[i] < most]
        mass, remaining = sum([loads[i] for i in candidates]), surplus
        for i in candidates:
            more = min(most - holding[i], max(1, remaining * loads[i] // mass), surplus)
            holding[i] = holding[i] + more
            surplus = surplus - more
    return np.array(holding)


def scatter_about(key, extent, scale, bound, cuts=(), kind=jnp.bfloat16):
    values = scale * jax.random.normal(key, extent, jnp.float32)
    if cuts:
        values = values * level_of(key, extent, cuts, -0.22, 0.18)
    return jnp.clip(values, -bound, bound).astype(kind)


def setup_inputs(seed: int = 0, part: int = 0) -> dict:
    seeds = jax.random.split(jax.random.key(seed), 10)
    part_splits = jax.random.split(jax.random.fold_in(seeds[9], part), 10)
    queries = draw_queries(jax.random.fold_in(jax.random.fold_in(seeds[9], part), 71), part)
    kv_pool = draw_kv_pool(jax.random.fold_in(jax.random.fold_in(seeds[9], part), 71), part)
    block_table = jax.random.permutation(part_splits[2], PAGES).astype(jnp.int32)
    lengths = uneven_parts(part_splits[3], SEQS, TOKENS, TOKENS // 2, 2).astype(jnp.int32)
    tokens_ffn = scatter_about(part_splits[4], (MTOKENS, D), 1.0, 6.0, ((0, 16),))
    routes_keys = jax.random.split(jax.random.fold_in(part_splits[5], 1), MTOKENS // M_DEV)
    routes_turns = jax.random.permutation(jax.random.fold_in(part_splits[5], 3), MTOKENS // M_DEV)
    routes = jax.vmap(lambda own, number: assign_block(jax.random.fold_in(part_splits[5], 2), own, number, M_DEV, EXPERTS, TOPK, CAP, 2))(routes_keys, routes_turns).reshape((MTOKENS, TOPK))
    route_probs = jnp.clip(0.1 + 0.9 * jax.random.uniform(part_splits[6], (MTOKENS, TOPK), jnp.float32) ** level_of(part_splits[6], (MTOKENS, TOPK), ((0, 16),), -0.2, 0.2), 0.1, 1.0)
    w_in = scatter_about(seeds[7], (N_TOK, EXP_GROUP, D, 2, UNITS), D ** -0.5, 0.09375, ((0, 16),))
    w_out = scatter_about(seeds[8], (N_TOK, EXP_GROUP, UNITS, D), HE ** -0.5, 0.125, ((0, 16),))
    return dict(queries=queries, kv_pool=kv_pool, block_table=block_table, lengths=lengths, tokens_ffn=tokens_ffn, routes=routes, route_probs=route_probs, w_in=w_in, w_out=w_out)


masked_score = -1e+30

def reference(queries, kv_pool, block_table, lengths, tokens_ffn, routes, route_probs, w_in, w_out):
    ends = jnp.cumsum(lengths).astype(jnp.int32)
    positions = jnp.arange(TOKENS, dtype=jnp.int32)
    requests = lax.optimization_barrier(jnp.sum((positions[:, None] >= ends[None, :]).astype(jnp.int32), axis=1))
    logical = kv_pool[block_table].reshape(TOKENS, 2 * HD)
    keys = logical[:, :HD]
    values = logical[:, HD:]
    visible = (requests[:, None] == requests[None, :]) & (positions[None, :] <= positions[:, None])
    per_head = jnp.transpose(queries.reshape(TOKENS, HEADS, HD), (1, 0, 2))

    def one_head(query_rows):
        scores = jnp.dot(query_rows, keys.T, preferred_element_type=jnp.float32) / jnp.sqrt(jnp.float32(HD))
        masked = jnp.where(visible, scores, masked_score)
        top = lax.optimization_barrier(jnp.max(masked, axis=1, keepdims=True))
        weights = jnp.where(visible, jnp.exp(scores - top), 0.0)
        totals = lax.optimization_barrier(jnp.sum(weights, axis=1, keepdims=True))
        summed = jnp.dot(weights.astype(jnp.bfloat16), values, preferred_element_type=jnp.float32)
        return (summed / totals).astype(jnp.bfloat16)
    heads_out = lax.map(one_head, per_head)
    attention = jnp.transpose(heads_out, (1, 0, 2)).reshape(TOKENS, HEADS * HD)
    groups = N_TOK // GROUP
    gate_all = w_in.reshape(groups, GROUP, EXP_GROUP, D, 2, UNITS).transpose(0, 2, 3, 4, 1, 5).reshape(EXPERTS, D, 2 * HE)
    down_all = w_out.reshape(groups, GROUP, EXP_GROUP, UNITS, D).transpose(0, 2, 1, 3, 4).reshape(EXPERTS, GROUP, UNITS, D)
    rows_all = N_TOK * CAP
    onehot = (routes[:, :, None] == jnp.arange(EXPERTS, dtype=jnp.int32)[None, None, :]).astype(jnp.int32)
    blocked = onehot.reshape(N_TOK, M_DEV * TOPK, EXPERTS)
    earlier = jnp.cumsum(blocked, axis=1) - blocked
    slot = lax.optimization_barrier(jnp.sum(earlier * blocked, axis=2)).reshape(MTOKENS, TOPK)
    source = jnp.arange(MTOKENS, dtype=jnp.int32) // M_DEV
    place = (source[:, None] * CAP + slot).astype(jnp.int32)

    def one_expert(carry, items):
        gate_up, down, expert = items
        hit = routes == expert
        where_row = lax.optimization_barrier(jnp.sum(jnp.where(hit, place, 0), axis=1)).astype(jnp.int32)
        weight = lax.optimization_barrier(jnp.sum(jnp.where(hit, route_probs, 0.0), axis=1))
        chosen = jnp.any(hit, axis=1)
        target = jnp.where(chosen, where_row, rows_all).astype(jnp.int32)
        rows_in = jnp.zeros((rows_all, D), jnp.bfloat16).at[target].set(tokens_ffn, mode='drop')
        pre = jnp.dot(rows_in, gate_up, preferred_element_type=jnp.float32).reshape(rows_all, 2, HE)
        hidden = (jax.nn.silu(pre[:, 0]) * pre[:, 1]).astype(jnp.bfloat16)
        pieces = jnp.einsum('rmu,mud->rmd', hidden.reshape(rows_all, GROUP, UNITS).astype(jnp.float32), down.astype(jnp.float32))
        result = lax.optimization_barrier(jnp.sum(pieces.astype(jnp.bfloat16).astype(jnp.float32), axis=1))
        taken = result[jnp.minimum(where_row, rows_all - 1)]
        return (carry + taken * weight[:, None], None)
    start = jnp.zeros((MTOKENS, D), jnp.float32)
    total, _ = lax.scan(one_expert, start, (gate_all, down_all, jnp.arange(EXPERTS, dtype=jnp.int32)))
    return (attention, total.astype(jnp.bfloat16))
```

```python
import functools
import math

import jax
import jax.numpy as jnp
from jax import lax
from jax.experimental import pallas as pl
from jax.experimental.pallas import tpu as pltpu
from jax.sharding import PartitionSpec as P

GROUP = 8


masked_score = -1e30


def attend_block(state, query_grid, query_pos, query_req, keys_vals, key_pos, key_req, scale):
    maxima, totals, summed = state
    head_dim = query_grid.shape[2]
    keys = keys_vals[:, :head_dim]
    values = keys_vals[:, head_dim:]
    scores = jnp.einsum("thd,sd->ths", query_grid, keys, preferred_element_type=jnp.float32) * scale
    visible = (query_req[:, None] == key_req[None, :]) & (key_pos[None, :] <= query_pos[:, None])
    visible = visible[:, None, :]
    fresh = jnp.maximum(maxima, jnp.max(jnp.where(visible, scores, masked_score), axis=2))
    weights = jnp.where(visible, jnp.exp(scores - fresh[:, :, None]), 0.0)
    factor = jnp.exp(maxima - fresh)
    totals = totals * factor + jnp.sum(weights, axis=2)
    summed = summed * factor[:, :, None] + jnp.einsum(
        "ths,sd->thd", weights.astype(jnp.bfloat16), values, preferred_element_type=jnp.float32
    )
    return (fresh, totals, summed)


def body(queries, kv_pool, block_table, lengths, tokens_ffn, routes, route_probs, w_in, w_out):
    page_rows = kv_pool.shape[1]
    head_dim = kv_pool.shape[2] // 2
    pages_all = block_table.shape[0]
    query_rows = queries.shape[0]
    head_count = queries.shape[1] // head_dim
    scale = 1.0 / math.sqrt(head_dim)
    ends = jnp.cumsum(lengths)
    query_pos = lax.axis_index("tok") * query_rows + jnp.arange(query_rows, dtype=jnp.int32)
    query_req = jnp.sum((query_pos[:, None] >= ends[None, :]).astype(jnp.int32), axis=1)
    page_ids = jnp.arange(pages_all, dtype=jnp.int32)
    inverse = jnp.sum(
        jnp.where(block_table[:, None] == page_ids[None, :], page_ids[:, None], 0), axis=0
    )
    query_grid = queries.reshape(query_rows, head_count, head_dim)
    in_page = jnp.arange(page_rows, dtype=jnp.int32)
    initial = (
        jnp.full((query_rows, head_count), masked_score, jnp.float32),
        jnp.zeros((query_rows, head_count), jnp.float32),
        jnp.zeros((query_rows, head_count, head_dim), jnp.float32),
    )
    state = initial
    piece = lax.all_gather(kv_pool, "tok", axis=0, tiled=True)
    count = piece.shape[0]
    group = max(1, 1024 // page_rows)
    for begin in range(0, count, group):
        size = min(group, count - begin)
        block = piece[begin : begin + size]
        logical = lax.dynamic_slice_in_dim(inverse, begin, size)
        key_pos = (logical[:, None] * page_rows + in_page[None, :]).reshape(-1)
        key_req = jnp.sum((key_pos[:, None] >= ends[None, :]).astype(jnp.int32), axis=1)
        state = attend_block(
            state,
            query_grid,
            query_pos,
            query_req,
            block.reshape(size * page_rows, 2 * head_dim),
            key_pos,
            key_req,
            scale,
        )
    maxima, totals, summed = state
    attention = (
        (summed / totals[:, :, None])
        .astype(jnp.bfloat16)
        .reshape(query_rows, head_count * head_dim)
    )
    devices_tok = lax.axis_size("tok")
    group_experts = w_in.shape[1]
    units = w_in.shape[4]
    groups = devices_tok // GROUP
    experts = group_experts * groups
    rows_here, top = routes.shape
    half_width = tokens_ffn.shape[1]
    capacity = min(rows_here, rows_here * top // experts + 1)
    flat = routes.reshape(-1)
    onehot = (flat[:, None] == jnp.arange(experts, dtype=jnp.int32)[None, :]).astype(jnp.int32)
    earlier = jnp.cumsum(onehot, axis=0) - onehot
    slot = jnp.sum(earlier * onehot, axis=1)
    destination = (flat // group_experts * capacity + slot) * group_experts + flat % group_experts
    dest_rows = destination.reshape(rows_here, top)
    slot_ids = jnp.arange(experts * capacity, dtype=jnp.int32)
    placing = jnp.any(slot_ids[:, None, None] == dest_rows[None, :, :], axis=2).astype(jnp.bfloat16)
    grouped = (
        jnp.dot(placing, tokens_ffn, preferred_element_type=jnp.float32)
        .astype(jnp.bfloat16)
        .reshape(groups, capacity, group_experts, half_width)
    )
    buffer = jnp.repeat(grouped, GROUP, axis=0)
    gate_up = w_in[0].reshape(group_experts, half_width, 2 * units)
    down = w_out[0]
    received = lax.all_to_all(buffer, "tok", split_axis=0, concat_axis=0, tiled=True)
    sources, count, local, width = received.shape
    pre = jnp.einsum(
        "snlw,lwk->snlk", received, gate_up, preferred_element_type=jnp.float32
    ).reshape(sources, count, local, 2, units)
    summed_pre = lax.psum(pre.astype(jnp.bfloat16), "sec").astype(jnp.float32)
    hidden = (jax.nn.silu(summed_pre[:, :, :, 0]) * summed_pre[:, :, :, 1]).astype(jnp.bfloat16)
    result = jnp.einsum("snlu,lud->snld", hidden, down, preferred_element_type=jnp.float32).astype(
        jnp.bfloat16
    )
    returned = lax.all_to_all(result, "tok", split_axis=0, concat_axis=0, tiled=True)
    combined = jnp.sum(
        returned.reshape(groups, GROUP, capacity, group_experts, half_width).astype(jnp.float32),
        axis=1,
    )
    picked = combined.reshape(experts * capacity, half_width)[destination].reshape(
        rows_here, top, half_width
    )
    moe_out = jnp.sum(picked * route_probs[:, :, None], axis=1).astype(jnp.bfloat16)
    return (attention, moe_out)


MESH = pl.DeviceIdType.MESH
LOG2E = 1.4426950408889634
TRANSPOSED = (((1,), (1,)), ((), ()))


def ring_tok(pos, chips, core):
    half = chips // 2
    chip = jnp.where(pos < half, 2 * pos, 2 * (chips - 1 - pos) + 1)
    return 2 * chip + core


def fused_kernel(
    chips,
    group_experts,
    units,
    wide,
    head_dim,
    x_ref,
    kv_ref,
    comb_ref,
    kpos_ref,
    start_ref,
    q_ref,
    w_ref,
    v_ref,
    att_ref,
    moe_ref,
    xg,
    kvg,
    pg,
    wbuf,
    vbuf,
    hid,
    mask,
    own,
    px,
    rr,
    local_sem,
    load_sem,
    ring_send,
    ring_recv,
    pair_send,
    pair_recv,
    px_send,
    px_recv,
    rr_send,
    rr_recv,
):
    rows, width = x_ref.shape
    kv_rows = kv_ref.shape[0]
    tok = lax.axis_index("tok")
    core = lax.rem(tok, 2)
    chip = tok // 2
    zed = chip // 2
    pos = jnp.where(lax.rem(chip, 2) == 0, zed, chips - 1 - zed)
    sign = 1 - 2 * core
    partner = tok + 1 - 2 * core
    after = ring_tok(lax.rem(pos + sign + chips, chips), chips, core)
    before = ring_tok(lax.rem(pos - sign + chips, chips), chips, core)

    def mine_at(step):
        return ring_tok(lax.rem(pos - sign * step + 2 * chips, chips), chips, core)

    def other_at(step):
        return ring_tok(lax.rem(pos + sign * step + 2 * chips, chips), chips, 1 - core)

    firsts = [
        pltpu.make_async_copy(x_ref, xg.at[tok], local_sem.at[0]),
        pltpu.make_async_copy(kv_ref, kvg.at[pl.ds(pl.multiple_of(tok * kv_rows, kv_rows), kv_rows)], local_sem.at[1]),
        pltpu.make_async_copy(comb_ref, pg.at[tok], local_sem.at[2]),
    ]
    for copy in firsts:
        copy.start()
    loads = []
    for l in range(group_experts):
        for j in range(2):
            loads.append(
                pltpu.make_async_copy(
                    w_ref.at[l, j], wbuf.at[l, pl.ds(j * wide, units)], load_sem.at[l * 3 + j]
                )
            )
        loads.append(
            pltpu.make_async_copy(v_ref.at[l], vbuf.at[pl.ds(l * wide, units)], load_sem.at[l * 3 + 2])
        )
    for copy in loads:
        copy.start()

    barrier = pltpu.get_barrier_semaphore()
    for device in (before, after, partner):
        pl.semaphore_signal(barrier, inc=1, device_id={"tok": device}, device_id_type=MESH)
    pl.semaphore_wait(barrier, 3)
    for copy in firsts:
        copy.wait()

    pieces = 2
    part_rows = rows // pieces

    def views(block):
        kv_at = pl.ds(pl.multiple_of(block * kv_rows, kv_rows), kv_rows)
        out = [kvg.at[kv_at], pg.at[block]]
        for i in range(pieces):
            out.append(xg.at[block, pl.ds(i * part_rows, part_rows)])
        return out

    def remote(ref, send, recv, device):
        return pltpu.make_async_remote_copy(
            src_ref=ref,
            dst_ref=ref,
            send_sem=send,
            recv_sem=recv,
            device_id={"tok": device},
            device_id_type=MESH,
        )

    def forward(step, wait, send):
        for i, ref in enumerate(views(mine_at(step))):
            if wait:
                remote(ref, ring_send.at[step, i], ring_recv.at[step, i], after).wait_recv()
            if send:
                remote(ref, ring_send.at[step, i], ring_recv.at[step + 1, i], after).start()
            remote(ref, pair_send.at[step, i], pair_recv.at[step, i], partner).start()

    def take_pair(step):
        for i, ref in enumerate(views(other_at(step))):
            remote(ref, pair_send.at[step, i], pair_recv.at[step, i], partner).wait_recv()

    first_expert = tok // GROUP * group_experts

    def up(step):
        a, b = mine_at(step), other_at(step)
        x = jnp.concatenate([xg[a], xg[b]], axis=0)
        scales = jnp.concatenate(
            [jnp.transpose(pg[a])[:rows], jnp.transpose(pg[b])[:rows]], axis=0
        )
        lanes = lax.broadcasted_iota(jnp.int32, scales.shape, 1)

        @pl.loop(0, group_experts)
        def _(l):
            pre = lax.dot_general(x, wbuf[l], TRANSPOSED, preferred_element_type=jnp.float32)
            gate, upper = pre[:, :wide], pre[:, wide:]
            scale = jnp.sum(jnp.where(lanes == first_expert + l, scales, 0.0), axis=1, keepdims=True)
            act = (gate / (1.0 + jnp.exp(-gate)) * upper * scale).astype(jnp.bfloat16)
            at = pl.ds(pl.multiple_of(l * wide, 128), wide)
            hid[a, :, at] = act[:rows]
            hid[b, :, at] = act[rows:]

    forward(0, False, True)

    spare = wide - units
    if spare:
        for l in range(group_experts):
            for j in range(2):
                wbuf[l, pl.ds(j * wide + units, spare)] = jnp.zeros((spare, width), wbuf.dtype)
            vbuf[pl.ds(l * wide + units, spare)] = jnp.zeros((spare, width), vbuf.dtype)
    key_pos = kpos_ref[...]
    first_pos = start_ref[...]
    query_rows = q_ref.shape[0]
    query_pos = tok * query_rows + lax.broadcasted_iota(jnp.int32, (query_rows, 1), 0)
    mask[...] = jnp.where((key_pos >= first_pos) & (key_pos <= query_pos), 0.0, -1e30)
    for copy in loads:
        copy.wait()

    @pl.loop(1, chips - 1)
    def _(step):
        forward(step, True, True)
        take_pair(step - 1)
        up(step - 1)

    forward(chips - 1, True, False)
    take_pair(chips - 2)
    up(chips - 2)
    take_pair(chips - 1)
    up(chips - 1)

    @pl.loop(0, chips)
    def _(step):
        for i, ref in enumerate(views(mine_at(step))):
            remote(ref, pair_send.at[step, i], pair_recv.at[step, i], partner).wait_send()

    @pl.loop(0, chips - 1)
    def _(step):
        for i, ref in enumerate(views(mine_at(step))):
            remote(ref, ring_send.at[step, i], ring_recv.at[step, i], after).wait_send()

    def px_copy(step):
        return pltpu.make_async_remote_copy(
            src_ref=xg.at[chips + step],
            dst_ref=px.at[step],
            send_sem=px_send.at[step],
            recv_sem=px_recv.at[step],
            device_id={"tok": partner},
            device_id_type=MESH,
        )

    halves = 2
    cut = width // halves

    def rr_copy(step, half):
        at = pl.ds(half * cut, cut)
        return pltpu.make_async_remote_copy(
            src_ref=xg.at[step, :, at],
            dst_ref=rr.at[step, :, at],
            send_sem=rr_send.at[step, half],
            recv_sem=rr_recv.at[step, half],
            device_id={"tok": after},
            device_id_type=MESH,
        )

    tile = 512 if width % 512 == 0 else 128

    def down(step):
        a, b = mine_at(step + 1), other_at(step + 1)
        h = jnp.concatenate([hid[a], hid[b]], axis=0)
        slot = lax.rem(step, 2)

        @pl.loop(0, width // tile)
        def _(n):
            at = pl.ds(pl.multiple_of(n * tile, tile), tile)
            part = jnp.dot(h, vbuf[:, at], preferred_element_type=jnp.float32)
            own[slot, :, at] = part[:rows]
            xg[chips + step, :, at] = part[rows:].astype(jnp.bfloat16)

        px_copy(step).start()

    heads = q_ref.shape[1] // head_dim
    together = 2 if heads % 2 == 0 else 1
    bundles = heads // together
    log_scale = LOG2E / math.sqrt(head_dim)

    def attend(bundle):
        at = [
            pl.ds(pl.multiple_of((bundle * together + i) * head_dim, head_dim), head_dim)
            for i in range(together)
        ]
        q = jnp.concatenate([q_ref[:, a] for a in at], axis=0)
        scores = lax.dot_general(
            q, kvg[:, :head_dim], TRANSPOSED, preferred_element_type=jnp.float32
        )
        hide = mask[...]
        scores = scores * log_scale + jnp.concatenate([hide] * together, axis=0)
        top = jnp.max(scores, axis=1, keepdims=True)
        weights = jnp.exp2(scores - top)
        total = jnp.sum(weights, axis=1, keepdims=True)
        summed = jnp.dot(
            weights.astype(jnp.bfloat16), kvg[:, head_dim:], preferred_element_type=jnp.float32
        )
        result = (summed / total).astype(jnp.bfloat16)
        for i, a in enumerate(at):
            att_ref[:, a] = result[i * query_rows : (i + 1) * query_rows]

    def pass_on(step, receive, last):
        px_copy(step).wait_recv()
        slot = lax.rem(step, 2)
        for half in range(halves):
            at = pl.ds(half * cut, cut)
            value = own[slot, :, at] + px[step, :, at].astype(jnp.float32)
            if receive:
                rr_copy(step - 1, half).wait_recv()
                value = value + rr[step - 1, :, at].astype(jnp.float32)
            if last:
                moe_ref[:, at] = value.astype(jnp.bfloat16)
            else:
                xg[step, :, at] = value.astype(jnp.bfloat16)
                rr_copy(step, half).start()

    def attend_share(step):
        @pl.loop(step * bundles // chips, (step + 1) * bundles // chips)
        def _(bundle):
            attend(bundle)

    down(0)
    down(1)
    pass_on(0, False, False)
    attend_share(0)

    @pl.loop(1, chips - 1)
    def _(step):
        down(step + 1)
        pass_on(step, True, False)
        attend_share(step)

    attend_share(chips - 1)
    pass_on(chips - 1, True, True)

    @pl.loop(0, chips)
    def _(step):
        px_copy(step).wait_send()

    @pl.loop(0, chips - 1)
    def _(step):
        for half in range(halves):
            rr_copy(step, half).wait_send()


def ring_body(queries, kv_pool, block_table, lengths, tokens_ffn, routes, route_probs, w_in, w_out):
    devices_tok = lax.axis_size("tok")
    chips = devices_tok // 2
    pages_here, page_rows, kv_width = kv_pool.shape
    head_dim = kv_width // 2
    pages_all = block_table.shape[0]
    keys_all = pages_all * page_rows
    query_rows = queries.shape[0]
    group_experts, units = w_in.shape[1], w_in.shape[4]
    experts = group_experts * (devices_tok // GROUP)
    rows, width = tokens_ffn.shape
    wide = -(-units // 128) * 128

    ends = jnp.cumsum(lengths)
    page_ids = jnp.arange(pages_all, dtype=jnp.int32)
    inverse = jnp.sum(
        jnp.where(block_table[:, None] == page_ids[None, :], page_ids[:, None], 0), axis=0
    )
    in_page = jnp.arange(page_rows, dtype=jnp.int32)
    key_pos = (inverse[:, None] * page_rows + in_page[None, :]).reshape(1, keys_all)
    query_pos = lax.axis_index("tok") * query_rows + jnp.arange(query_rows, dtype=jnp.int32)
    starts = jnp.max(jnp.where(query_pos[:, None] >= ends[None, :], ends[None, :], 0), axis=1)[:, None]

    expert_rows = -(-experts // 8) * 8
    token_lanes = -(-rows // 128) * 128
    expert_ids = jnp.arange(expert_rows, dtype=jnp.int32)
    combine = jnp.sum(
        jnp.where(routes.T[None] == expert_ids[:, None, None], route_probs.T[None], 0.0), axis=1
    )
    combine = jnp.pad(combine, ((0, 0), (0, token_lanes - rows)))

    gate_up = jnp.transpose(w_in[0], (0, 2, 3, 1))
    any_spec = pl.BlockSpec(memory_space=pl.ANY)
    vmem = pl.BlockSpec(memory_space=pltpu.VMEM)
    dma = pltpu.SemaphoreType.DMA
    bf16 = jnp.bfloat16
    kernel = functools.partial(fused_kernel, chips, group_experts, units, wide, head_dim)
    return pl.pallas_call(
        kernel,
        out_shape=(
            jax.ShapeDtypeStruct(queries.shape, bf16),
            jax.ShapeDtypeStruct(tokens_ffn.shape, bf16),
        ),
        in_specs=[any_spec, any_spec, any_spec, vmem, vmem, vmem, any_spec, any_spec],
        out_specs=(vmem, vmem),
        scratch_shapes=[
            pltpu.VMEM((devices_tok, rows, width), bf16),
            pltpu.VMEM((keys_all, kv_width), bf16),
            pltpu.VMEM((devices_tok, expert_rows, token_lanes), jnp.float32),
            pltpu.VMEM((group_experts, 2 * wide, width), bf16),
            pltpu.VMEM((group_experts * wide, width), bf16),
            pltpu.VMEM((devices_tok, rows, group_experts * wide), bf16),
            pltpu.VMEM((query_rows, keys_all), jnp.float32),
            pltpu.VMEM((2, rows, width), jnp.float32),
            pltpu.VMEM((chips, rows, width), bf16),
            pltpu.VMEM((chips - 1, rows, width), bf16),
            dma((3,)),
            dma((group_experts * 3,)),
            dma((chips, 4)),
            dma((chips, 4)),
            dma((chips, 4)),
            dma((chips, 4)),
            dma((chips,)),
            dma((chips,)),
            dma((chips - 1, 2)),
            dma((chips - 1, 2)),
        ],
        compiler_params=pltpu.CompilerParams(
            collective_id=0, has_side_effects=True, vmem_limit_bytes=60 * 1024 * 1024
        ),
    )(
        tokens_ffn,
        kv_pool.reshape(pages_here * page_rows, kv_width),
        combine,
        key_pos,
        starts,
        queries,
        gate_up,
        w_out[0],
    )


def solution(mesh):
    ring = mesh.shape["sec"] == 1 and mesh.shape["tok"] % 8 == 0
    chosen = ring_body if ring else body

    in_specs = (
        P(("replica", "tok"), "sec"),
        P(("replica", "tok"), None, None),
        P("replica"),
        P("replica"),
        P(("replica", "tok"), "sec"),
        P(("replica", "tok"), None),
        P(("replica", "tok"), None),
        P("tok", None, "sec", None, None),
        P("tok", None, None, "sec"),
    )
    out_specs = (P(("replica", "tok"), "sec"), P(("replica", "tok"), "sec"))
    return jax.shard_map(chosen, mesh=mesh, in_specs=in_specs, out_specs=out_specs, check_vma=False)
```

```python
import functools
import math

import jax
import jax.numpy as jnp
from jax import lax
from jax.experimental import pallas as pl
from jax.experimental.pallas import tpu as pltpu
from jax.sharding import PartitionSpec as P

GROUP = 8


masked_score = -1e30


def attend_block(state, query_grid, query_pos, query_req, keys_vals, key_pos, key_req, scale):
    maxima, totals, summed = state
    head_dim = query_grid.shape[2]
    keys = keys_vals[:, :head_dim]
    values = keys_vals[:, head_dim:]
    scores = jnp.einsum("thd,sd->ths", query_grid, keys, preferred_element_type=jnp.float32) * scale
    visible = (query_req[:, None] == key_req[None, :]) & (key_pos[None, :] <= query_pos[:, None])
    visible = visible[:, None, :]
    fresh = jnp.maximum(maxima, jnp.max(jnp.where(visible, scores, masked_score), axis=2))
    weights = jnp.where(visible, jnp.exp(scores - fresh[:, :, None]), 0.0)
    factor = jnp.exp(maxima - fresh)
    totals = totals * factor + jnp.sum(weights, axis=2)
    summed = summed * factor[:, :, None] + jnp.einsum(
        "ths,sd->thd", weights.astype(jnp.bfloat16), values, preferred_element_type=jnp.float32
    )
    return (fresh, totals, summed)


def body(queries, kv_pool, block_table, lengths, tokens_ffn, routes, route_probs, w_in, w_out):
    page_rows = kv_pool.shape[1]
    head_dim = kv_pool.shape[2] // 2
    pages_all = block_table.shape[0]
    query_rows = queries.shape[0]
    head_count = queries.shape[1] // head_dim
    scale = 1.0 / math.sqrt(head_dim)
    ends = jnp.cumsum(lengths)
    query_pos = lax.axis_index("tok") * query_rows + jnp.arange(query_rows, dtype=jnp.int32)
    query_req = jnp.sum((query_pos[:, None] >= ends[None, :]).astype(jnp.int32), axis=1)
    page_ids = jnp.arange(pages_all, dtype=jnp.int32)
    inverse = jnp.sum(
        jnp.where(block_table[:, None] == page_ids[None, :], page_ids[:, None], 0), axis=0
    )
    query_grid = queries.reshape(query_rows, head_count, head_dim)
    in_page = jnp.arange(page_rows, dtype=jnp.int32)
    initial = (
        jnp.full((query_rows, head_count), masked_score, jnp.float32),
        jnp.zeros((query_rows, head_count), jnp.float32),
        jnp.zeros((query_rows, head_count, head_dim), jnp.float32),
    )
    state = initial
    piece = lax.all_gather(kv_pool, "tok", axis=0, tiled=True)
    count = piece.shape[0]
    group = max(1, 1024 // page_rows)
    for begin in range(0, count, group):
        size = min(group, count - begin)
        block = piece[begin : begin + size]
        logical = lax.dynamic_slice_in_dim(inverse, begin, size)
        key_pos = (logical[:, None] * page_rows + in_page[None, :]).reshape(-1)
        key_req = jnp.sum((key_pos[:, None] >= ends[None, :]).astype(jnp.int32), axis=1)
        state = attend_block(
            state,
            query_grid,
            query_pos,
            query_req,
            block.reshape(size * page_rows, 2 * head_dim),
            key_pos,
            key_req,
            scale,
        )
    maxima, totals, summed = state
    attention = (
        (summed / totals[:, :, None])
        .astype(jnp.bfloat16)
        .reshape(query_rows, head_count * head_dim)
    )
    devices_tok = lax.axis_size("tok")
    group_experts = w_in.shape[1]
    units = w_in.shape[4]
    groups = devices_tok // GROUP
    experts = group_experts * groups
    rows_here, top = routes.shape
    half_width = tokens_ffn.shape[1]
    capacity = min(rows_here, rows_here * top // experts + 1)
    flat = routes.reshape(-1)
    onehot = (flat[:, None] == jnp.arange(experts, dtype=jnp.int32)[None, :]).astype(jnp.int32)
    earlier = jnp.cumsum(onehot, axis=0) - onehot
    slot = jnp.sum(earlier * onehot, axis=1)
    destination = (flat // group_experts * capacity + slot) * group_experts + flat % group_experts
    dest_rows = destination.reshape(rows_here, top)
    slot_ids = jnp.arange(experts * capacity, dtype=jnp.int32)
    placing = jnp.any(slot_ids[:, None, None] == dest_rows[None, :, :], axis=2).astype(jnp.bfloat16)
    grouped = (
        jnp.dot(placing, tokens_ffn, preferred_element_type=jnp.float32)
        .astype(jnp.bfloat16)
        .reshape(groups, capacity, group_experts, half_width)
    )
    buffer = jnp.repeat(grouped, GROUP, axis=0)
    gate_up = w_in[0].reshape(group_experts, half_width, 2 * units)
    down = w_out[0]
    received = lax.all_to_all(buffer, "tok", split_axis=0, concat_axis=0, tiled=True)
    sources, count, local, width = received.shape
    pre = jnp.einsum(
        "snlw,lwk->snlk", received, gate_up, preferred_element_type=jnp.float32
    ).reshape(sources, count, local, 2, units)
    summed_pre = lax.psum(pre.astype(jnp.bfloat16), "sec").astype(jnp.float32)
    hidden = (jax.nn.silu(summed_pre[:, :, :, 0]) * summed_pre[:, :, :, 1]).astype(jnp.bfloat16)
    result = jnp.einsum("snlu,lud->snld", hidden, down, preferred_element_type=jnp.float32).astype(
        jnp.bfloat16
    )
    returned = lax.all_to_all(result, "tok", split_axis=0, concat_axis=0, tiled=True)
    combined = jnp.sum(
        returned.reshape(groups, GROUP, capacity, group_experts, half_width).astype(jnp.float32),
        axis=1,
    )
    picked = combined.reshape(experts * capacity, half_width)[destination].reshape(
        rows_here, top, half_width
    )
    moe_out = jnp.sum(picked * route_probs[:, :, None], axis=1).astype(jnp.bfloat16)
    return (attention, moe_out)


MESH = pl.DeviceIdType.MESH
LOG2E = 1.4426950408889634
TRANSPOSED = (((1,), (1,)), ((), ()))


def ring_tok(pos, chips, core):
    half = chips // 2
    chip = jnp.where(pos < half, 2 * pos, 2 * (chips - 1 - pos) + 1)
    return 2 * chip + core


def fused_kernel(
    chips,
    group_experts,
    units,
    head_dim,
    page_rows,
    x_ref,
    kv_ref,
    routes_ref,
    probs_ref,
    table_ref,
    lengths_ref,
    q_ref,
    w_ref,
    v_ref,
    att_ref,
    moe_ref,
    xg,
    kvg,
    pg,
    wbuf,
    vbuf,
    hid,
    mask,
    keys,
    rows_of_values,
    vals,
    own,
    pstage,
    rstage,
    px,
    rr,
    local_sem,
    load_sem,
    ring_send,
    ring_recv,
    pair_send,
    pair_recv,
    px_send,
    px_recv,
    rr_send,
    rr_recv,
):
    rows, width = x_ref.shape
    kv_pages = kv_ref.shape[0]
    tok = lax.axis_index("tok")
    core = lax.rem(tok, 2)
    chip = tok // 2
    zed = chip // 2
    pos = jnp.where(lax.rem(chip, 2) == 0, zed, chips - 1 - zed)
    sign = 1 - 2 * core
    partner = tok + 1 - 2 * core
    after = ring_tok(lax.rem(pos + sign + chips, chips), chips, core)
    before = ring_tok(lax.rem(pos - sign + chips, chips), chips, core)

    def mine_at(step):
        return ring_tok(lax.rem(pos - sign * step + 2 * chips, chips), chips, core)

    def other_at(step):
        return ring_tok(lax.rem(pos + sign * step + 2 * chips, chips), chips, 1 - core)

    firsts = [
        pltpu.make_async_copy(x_ref, xg.at[tok], local_sem.at[0]),
        pltpu.make_async_copy(kv_ref, kvg.at[pl.ds(tok * kv_pages, kv_pages)], local_sem.at[1]),
    ]
    for copy in firsts:
        copy.start()
    loads = []
    for l in range(group_experts):
        for j in range(2):
            loads.append(
                pltpu.make_async_copy(
                    w_ref.at[l, j], wbuf.at[l, pl.ds(j * units, units)], load_sem.at[l * 3 + j]
                )
            )
        loads.append(
            pltpu.make_async_copy(v_ref.at[l], vbuf.at[pl.ds(l * units, units)], load_sem.at[l * 3 + 2])
        )
    for copy in loads:
        copy.start()

    names = routes_ref[...]
    probs = probs_ref[...]
    expert_ids = lax.broadcasted_iota(jnp.int32, (pg.shape[1], rows), 0)
    combine = jnp.zeros(expert_ids.shape, jnp.float32)
    for k in range(names.shape[0]):
        combine = combine + jnp.where(names[k : k + 1] == expert_ids, probs[k : k + 1], 0.0)
    pg[tok] = jnp.concatenate(
        [jnp.where(core == 0, combine, 0.0), jnp.where(core == 1, combine, 0.0)], axis=1
    )

    barrier = pltpu.get_barrier_semaphore()
    for device in (before, after, partner):
        pl.semaphore_signal(barrier, inc=1, device_id={"tok": device}, device_id_type=MESH)
    pl.semaphore_wait(barrier, 3)
    for copy in firsts:
        copy.wait()

    pieces = 2
    part_rows = rows // pieces

    def views(block):
        out = [kvg.at[pl.ds(block * kv_pages, kv_pages)], pg.at[block]]
        for i in range(pieces):
            out.append(xg.at[block, pl.ds(i * part_rows, part_rows)])
        return out

    def remote(ref, send, recv, device):
        return pltpu.make_async_remote_copy(
            src_ref=ref,
            dst_ref=ref,
            send_sem=send,
            recv_sem=recv,
            device_id={"tok": device},
            device_id_type=MESH,
        )

    def forward(step, wait, send):
        for i, ref in enumerate(views(mine_at(step))):
            if wait:
                remote(ref, ring_send.at[step, i], ring_recv.at[step, i], after).wait_recv()
            if send:
                remote(ref, ring_send.at[step, i], ring_recv.at[step + 1, i], after).start()
            remote(ref, pair_send.at[step, i], pair_recv.at[step, i], partner).start()

    def take_pair(step):
        for i, ref in enumerate(views(other_at(step))):
            remote(ref, pair_send.at[step, i], pair_recv.at[step, i], partner).wait_recv()

    first_expert = tok // GROUP * group_experts

    def up(step):
        mine, other = mine_at(step), other_at(step)
        a = jnp.where(core == 0, mine, other)
        b = jnp.where(core == 0, other, mine)
        x = jnp.concatenate([xg[a], xg[b]], axis=0)
        scales = pg[a] + pg[b]
        experts_at = lax.broadcasted_iota(jnp.int32, scales.shape, 0)

        @pl.loop(0, group_experts)
        def _(l):
            pre = lax.dot_general(wbuf[l], x, TRANSPOSED, preferred_element_type=jnp.float32)
            gate, upper = pre[:units], pre[units:]
            scale = jnp.sum(
                jnp.where(experts_at == first_expert + l, scales, 0.0), axis=0, keepdims=True
            )
            act = (gate / (1.0 + jnp.exp(-gate)) * upper * scale).astype(jnp.bfloat16)
            hid[step, pl.ds(pl.multiple_of(l * units, units), units)] = act

    forward(0, False, True)

    query_rows = q_ref.shape[0]
    window = mask.shape[0]
    base = jnp.maximum(tok * query_rows + query_rows - window, 0)
    query_pos = tok * query_rows + lax.broadcasted_iota(jnp.int32, (1, query_rows), 1)
    first_pos = jnp.zeros_like(query_pos)
    end = jnp.int32(0)
    for i in range(lengths_ref.shape[0]):
        end = end + lengths_ref[i]
        first_pos = jnp.where(query_pos >= end, end, first_pos)
    key_pos = base + lax.broadcasted_iota(jnp.int32, (window, 1), 0)
    mask[...] = jnp.where((key_pos >= first_pos) & (key_pos <= query_pos), 0.0, -1e30)
    forward(1, True, True)
    take_pair(0)
    for copy in loads:
        copy.wait()
    up(0)

    @pl.loop(2, chips - 1)
    def _(step):
        forward(step, True, True)
        take_pair(step - 1)
        up(step - 1)

    def px_copy(step):
        return pltpu.make_async_remote_copy(
            src_ref=pstage.at[lax.rem(step, 2)],
            dst_ref=px.at[step],
            send_sem=px_send.at[step],
            recv_sem=px_recv.at[step],
            device_id={"tok": partner},
            device_id_type=MESH,
        )

    halves = 2
    cut = width // halves

    def rr_copy(step, half):
        at = pl.ds(half * cut, cut)
        return pltpu.make_async_remote_copy(
            src_ref=rstage.at[lax.rem(step, 2), :, at],
            dst_ref=rr.at[step, :, at],
            send_sem=rr_send.at[step, half],
            recv_sem=rr_recv.at[step, half],
            device_id={"tok": after},
            device_id_type=MESH,
        )

    tile = 512 if width % 512 == 0 else 128

    def down(step, reuse):
        if reuse:
            px_copy(step - 2).wait_send()
        h = jnp.transpose(hid[lax.rem(step + 1, chips)])
        slot = lax.rem(step, 2)

        @pl.loop(0, width // tile)
        def _(n):
            at = pl.ds(pl.multiple_of(n * tile, tile), tile)
            part = jnp.dot(h, vbuf[:, at], preferred_element_type=jnp.float32)
            first, second = part[:rows], part[rows:]
            own[slot, :, at] = jnp.where(core == 0, first, second)
            pstage[slot, :, at] = jnp.where(core == 0, second, first).astype(jnp.bfloat16)

        px_copy(step).start()

    heads = q_ref.shape[1] // head_dim
    together = 2 if heads % 2 == 0 else 1
    bundles = heads // together
    log_scale = LOG2E / math.sqrt(head_dim)

    def attend(bundle):
        at = [
            pl.ds(pl.multiple_of((bundle * together + i) * head_dim, head_dim), head_dim)
            for i in range(together)
        ]
        q = jnp.concatenate([q_ref[:, a] for a in at], axis=0)
        scores = lax.dot_general(
            keys[...], q, TRANSPOSED, preferred_element_type=jnp.float32
        )
        hide = mask[...]
        scores = scores * log_scale + jnp.concatenate([hide] * together, axis=1)
        top = jnp.max(scores, axis=0, keepdims=True)
        weights = jnp.exp2(scores - top)
        total = jnp.sum(weights, axis=0, keepdims=True)
        summed = jnp.dot(vals[...], weights.astype(jnp.bfloat16), preferred_element_type=jnp.float32)
        result = jnp.transpose(summed / total).astype(jnp.bfloat16)
        for i, a in enumerate(at):
            att_ref[:, a] = result[i * query_rows : (i + 1) * query_rows]

    def pass_on(step, receive, reuse, last):
        px_copy(step).wait_recv()
        slot = lax.rem(step, 2)
        for half in range(halves):
            at = pl.ds(half * cut, cut)
            value = own[slot, :, at] + px[step, :, at].astype(jnp.float32)
            if receive:
                rr_copy(step - 1, half).wait_recv()
                value = value + rr[step - 1, :, at].astype(jnp.float32)
            if reuse:
                rr_copy(step - 2, half).wait_send()
            if last:
                moe_ref[:, at] = value.astype(jnp.bfloat16)
            else:
                rstage[slot, :, at] = value.astype(jnp.bfloat16)
                rr_copy(step, half).start()

    down(0, False)
    forward(chips - 1, True, False)
    pass_on(0, False, False, False)
    down(1, False)
    take_pair(chips - 2)
    up(chips - 2)
    pass_on(1, True, False, False)
    down(2, True)
    take_pair(chips - 1)
    up(chips - 1)

    @pl.loop(0, window // page_rows)
    def _(i):
        page = table_ref[base // page_rows + i]
        block = kvg[page]
        at = pl.ds(pl.multiple_of(i * page_rows, page_rows), page_rows)
        keys[at, :] = block[:, :head_dim]
        rows_of_values[at, :] = block[:, head_dim:]

    vals[...] = jnp.transpose(rows_of_values[...])
    spans = chips - 3

    @pl.loop(2, chips - 1)
    def _(step):
        pass_on(step, True, True, False)
        down(step + 1, True)

        @pl.loop((step - 2) * bundles // spans, (step - 1) * bundles // spans)
        def _(bundle):
            attend(bundle)

    pass_on(chips - 1, True, True, True)

    for step in (chips - 2, chips - 1):
        px_copy(step).wait_send()
    for half in range(halves):
        rr_copy(chips - 2, half).wait_send()

    @pl.loop(0, chips)
    def _(step):
        for i, ref in enumerate(views(mine_at(step))):
            remote(ref, pair_send.at[step, i], pair_recv.at[step, i], partner).wait_send()

    @pl.loop(0, chips - 1)
    def _(step):
        for i, ref in enumerate(views(mine_at(step))):
            remote(ref, ring_send.at[step, i], ring_recv.at[step, i], after).wait_send()


def ring_body(queries, kv_pool, block_table, lengths, tokens_ffn, routes, route_probs, w_in, w_out):
    devices_tok = lax.axis_size("tok")
    chips = devices_tok // 2
    _, page_rows, kv_width = kv_pool.shape
    head_dim = kv_width // 2
    pages_all = block_table.shape[0]
    keys_all = pages_all * page_rows
    query_rows = queries.shape[0]
    group_experts, units = w_in.shape[1], w_in.shape[4]
    experts = group_experts * (devices_tok // GROUP)
    rows, width = tokens_ffn.shape

    expert_rows = -(-experts // 8) * 8
    window = min(keys_all, keys_all // 2 + query_rows)
    gate_up = jnp.transpose(w_in[0], (0, 2, 3, 1))
    any_spec = pl.BlockSpec(memory_space=pl.ANY)
    vmem = pl.BlockSpec(memory_space=pltpu.VMEM)
    smem = pl.BlockSpec(memory_space=pltpu.SMEM)
    dma = pltpu.SemaphoreType.DMA
    bf16 = jnp.bfloat16
    kernel = functools.partial(fused_kernel, chips, group_experts, units, head_dim, page_rows)
    return pl.pallas_call(
        kernel,
        out_shape=(
            jax.ShapeDtypeStruct(queries.shape, bf16),
            jax.ShapeDtypeStruct(tokens_ffn.shape, bf16),
        ),
        in_specs=[any_spec, any_spec, vmem, vmem, smem, smem, vmem, any_spec, any_spec],
        out_specs=(vmem, vmem),
        scratch_shapes=[
            pltpu.VMEM((devices_tok, rows, width), bf16),
            pltpu.VMEM((pages_all, page_rows, kv_width), bf16),
            pltpu.VMEM((devices_tok, expert_rows, 2 * rows), jnp.float32),
            pltpu.VMEM((group_experts, 2 * units, width), bf16),
            pltpu.VMEM((group_experts * units, width), bf16),
            pltpu.VMEM((chips, group_experts * units, 2 * rows), bf16),
            pltpu.VMEM((window, query_rows), jnp.float32),
            pltpu.VMEM((window, head_dim), bf16),
            pltpu.VMEM((window, head_dim), bf16),
            pltpu.VMEM((head_dim, window), bf16),
            pltpu.VMEM((2, rows, width), jnp.float32),
            pltpu.VMEM((2, rows, width), bf16),
            pltpu.VMEM((2, rows, width), bf16),
            pltpu.VMEM((chips, rows, width), bf16),
            pltpu.VMEM((chips - 1, rows, width), bf16),
            dma((2,)),
            dma((group_experts * 3,)),
            dma((chips, 4)),
            dma((chips, 4)),
            dma((chips, 4)),
            dma((chips, 4)),
            dma((chips,)),
            dma((chips,)),
            dma((chips - 1, 2)),
            dma((chips - 1, 2)),
        ],
        compiler_params=pltpu.CompilerParams(
            collective_id=0, has_side_effects=True, vmem_limit_bytes=60 * 1024 * 1024
        ),
    )(
        tokens_ffn,
        kv_pool,
        routes.T,
        route_probs.T,
        block_table,
        lengths,
        queries,
        gate_up,
        w_out[0],
    )


def solution(mesh):
    ring = mesh.shape["sec"] == 1 and mesh.shape["tok"] % 8 == 0
    chosen = ring_body if ring else body

    in_specs = (
        P(("replica", "tok"), "sec"),
        P(("replica", "tok"), None, None),
        P("replica"),
        P("replica"),
        P(("replica", "tok"), "sec"),
        P(("replica", "tok"), None),
        P(("replica", "tok"), None),
        P("tok", None, "sec", None, None),
        P("tok", None, None, "sec"),
    )
    out_specs = (P(("replica", "tok"), "sec"), P(("replica", "tok"), "sec"))
    return jax.shard_map(chosen, mesh=mesh, in_specs=in_specs, out_specs=out_specs, check_vma=False)
```

```python
import functools
import math

import jax
import jax.numpy as jnp
from jax import lax
from jax.experimental import pallas as pl
from jax.experimental.pallas import tpu as pltpu
from jax.sharding import PartitionSpec as P

GROUP = 8


masked_score = -1e30


def attend_block(state, query_grid, query_pos, query_req, keys_vals, key_pos, key_req, scale):
    maxima, totals, summed = state
    head_dim = query_grid.shape[2]
    keys = keys_vals[:, :head_dim]
    values = keys_vals[:, head_dim:]
    scores = jnp.einsum("thd,sd->ths", query_grid, keys, preferred_element_type=jnp.float32) * scale
    visible = (query_req[:, None] == key_req[None, :]) & (key_pos[None, :] <= query_pos[:, None])
    visible = visible[:, None, :]
    fresh = jnp.maximum(maxima, jnp.max(jnp.where(visible, scores, masked_score), axis=2))
    weights = jnp.where(visible, jnp.exp(scores - fresh[:, :, None]), 0.0)
    factor = jnp.exp(maxima - fresh)
    totals = totals * factor + jnp.sum(weights, axis=2)
    summed = summed * factor[:, :, None] + jnp.einsum(
        "ths,sd->thd", weights.astype(jnp.bfloat16), values, preferred_element_type=jnp.float32
    )
    return (fresh, totals, summed)


def body(queries, kv_pool, block_table, lengths, tokens_ffn, routes, route_probs, w_in, w_out):
    page_rows = kv_pool.shape[1]
    head_dim = kv_pool.shape[2] // 2
    pages_all = block_table.shape[0]
    query_rows = queries.shape[0]
    head_count = queries.shape[1] // head_dim
    scale = 1.0 / math.sqrt(head_dim)
    ends = jnp.cumsum(lengths)
    query_pos = lax.axis_index("tok") * query_rows + jnp.arange(query_rows, dtype=jnp.int32)
    query_req = jnp.sum((query_pos[:, None] >= ends[None, :]).astype(jnp.int32), axis=1)
    page_ids = jnp.arange(pages_all, dtype=jnp.int32)
    inverse = jnp.sum(
        jnp.where(block_table[:, None] == page_ids[None, :], page_ids[:, None], 0), axis=0
    )
    query_grid = queries.reshape(query_rows, head_count, head_dim)
    in_page = jnp.arange(page_rows, dtype=jnp.int32)
    initial = (
        jnp.full((query_rows, head_count), masked_score, jnp.float32),
        jnp.zeros((query_rows, head_count), jnp.float32),
        jnp.zeros((query_rows, head_count, head_dim), jnp.float32),
    )
    state = initial
    piece = lax.all_gather(kv_pool, "tok", axis=0, tiled=True)
    count = piece.shape[0]
    group = max(1, 1024 // page_rows)
    for begin in range(0, count, group):
        size = min(group, count - begin)
        block = piece[begin : begin + size]
        logical = lax.dynamic_slice_in_dim(inverse, begin, size)
        key_pos = (logical[:, None] * page_rows + in_page[None, :]).reshape(-1)
        key_req = jnp.sum((key_pos[:, None] >= ends[None, :]).astype(jnp.int32), axis=1)
        state = attend_block(
            state,
            query_grid,
            query_pos,
            query_req,
            block.reshape(size * page_rows, 2 * head_dim),
            key_pos,
            key_req,
            scale,
        )
    maxima, totals, summed = state
    attention = (
        (summed / totals[:, :, None])
        .astype(jnp.bfloat16)
        .reshape(query_rows, head_count * head_dim)
    )
    devices_tok = lax.axis_size("tok")
    group_experts = w_in.shape[1]
    units = w_in.shape[4]
    groups = devices_tok // GROUP
    experts = group_experts * groups
    rows_here, top = routes.shape
    half_width = tokens_ffn.shape[1]
    capacity = min(rows_here, rows_here * top // experts + 1)
    flat = routes.reshape(-1)
    onehot = (flat[:, None] == jnp.arange(experts, dtype=jnp.int32)[None, :]).astype(jnp.int32)
    earlier = jnp.cumsum(onehot, axis=0) - onehot
    slot = jnp.sum(earlier * onehot, axis=1)
    destination = (flat // group_experts * capacity + slot) * group_experts + flat % group_experts
    dest_rows = destination.reshape(rows_here, top)
    slot_ids = jnp.arange(experts * capacity, dtype=jnp.int32)
    placing = jnp.any(slot_ids[:, None, None] == dest_rows[None, :, :], axis=2).astype(jnp.bfloat16)
    grouped = (
        jnp.dot(placing, tokens_ffn, preferred_element_type=jnp.float32)
        .astype(jnp.bfloat16)
        .reshape(groups, capacity, group_experts, half_width)
    )
    buffer = jnp.repeat(grouped, GROUP, axis=0)
    gate_up = w_in[0].reshape(group_experts, half_width, 2 * units)
    down = w_out[0]
    received = lax.all_to_all(buffer, "tok", split_axis=0, concat_axis=0, tiled=True)
    sources, count, local, width = received.shape
    pre = jnp.einsum(
        "snlw,lwk->snlk", received, gate_up, preferred_element_type=jnp.float32
    ).reshape(sources, count, local, 2, units)
    summed_pre = lax.psum(pre.astype(jnp.bfloat16), "sec").astype(jnp.float32)
    hidden = (jax.nn.silu(summed_pre[:, :, :, 0]) * summed_pre[:, :, :, 1]).astype(jnp.bfloat16)
    result = jnp.einsum("snlu,lud->snld", hidden, down, preferred_element_type=jnp.float32).astype(
        jnp.bfloat16
    )
    returned = lax.all_to_all(result, "tok", split_axis=0, concat_axis=0, tiled=True)
    combined = jnp.sum(
        returned.reshape(groups, GROUP, capacity, group_experts, half_width).astype(jnp.float32),
        axis=1,
    )
    picked = combined.reshape(experts * capacity, half_width)[destination].reshape(
        rows_here, top, half_width
    )
    moe_out = jnp.sum(picked * route_probs[:, :, None], axis=1).astype(jnp.bfloat16)
    return (attention, moe_out)


MESH = pl.DeviceIdType.MESH
LOG2E = 1.4426950408889634
TRANSPOSED = (((1,), (1,)), ((), ()))


def ring_tok(pos, chips, core):
    half = chips // 2
    chip = jnp.where(pos < half, 2 * pos, 2 * (chips - 1 - pos) + 1)
    return 2 * chip + core


def fused_kernel(
    chips,
    group_experts,
    units,
    head_dim,
    page_rows,
    x_ref,
    kv_ref,
    routes_ref,
    probs_ref,
    table_ref,
    lengths_ref,
    q_ref,
    w_ref,
    v_ref,
    att_ref,
    moe_ref,
    xg,
    kvg,
    pg,
    wbuf,
    vbuf,
    hid,
    mask,
    keys,
    rows_of_values,
    vals,
    own,
    pstage,
    rstage,
    px,
    rr,
    local_sem,
    load_sem,
    ring_send,
    ring_recv,
    pair_send,
    pair_recv,
    px_send,
    px_recv,
    rr_send,
    rr_recv,
):
    rows, width = x_ref.shape
    kv_pages = kv_ref.shape[0]
    tok = lax.axis_index("tok")
    core = lax.rem(tok, 2)
    chip = tok // 2
    zed = chip // 2
    pos = jnp.where(lax.rem(chip, 2) == 0, zed, chips - 1 - zed)
    sign = 1 - 2 * core
    partner = tok + 1 - 2 * core
    after = ring_tok(lax.rem(pos + sign + chips, chips), chips, core)
    before = ring_tok(lax.rem(pos - sign + chips, chips), chips, core)

    def mine_at(step):
        return ring_tok(lax.rem(pos - sign * step + 2 * chips, chips), chips, core)

    def other_at(step):
        return ring_tok(lax.rem(pos + sign * step + 2 * chips, chips), chips, 1 - core)

    firsts = [
        pltpu.make_async_copy(x_ref, xg.at[tok], local_sem.at[0]),
        pltpu.make_async_copy(kv_ref, kvg.at[pl.ds(tok * kv_pages, kv_pages)], local_sem.at[1]),
    ]
    for copy in firsts:
        copy.start()
    loads = []
    for l in range(group_experts):
        for j in range(2):
            loads.append(
                pltpu.make_async_copy(
                    w_ref.at[l, j], wbuf.at[l, pl.ds(j * units, units)], load_sem.at[l * 3 + j]
                )
            )
        loads.append(
            pltpu.make_async_copy(v_ref.at[l], vbuf.at[pl.ds(l * units, units)], load_sem.at[l * 3 + 2])
        )
    for copy in loads:
        copy.start()

    names = routes_ref[...]
    probs = probs_ref[...]
    expert_ids = lax.broadcasted_iota(jnp.int32, (pg.shape[1], rows), 0)
    combine = jnp.zeros(expert_ids.shape, jnp.float32)
    for k in range(names.shape[0]):
        combine = combine + jnp.where(names[k : k + 1] == expert_ids, probs[k : k + 1], 0.0)
    pg[tok] = jnp.concatenate(
        [jnp.where(core == 0, combine, 0.0), jnp.where(core == 1, combine, 0.0)], axis=1
    )

    barrier = pltpu.get_barrier_semaphore()
    for device in (before, after, partner):
        pl.semaphore_signal(barrier, inc=1, device_id={"tok": device}, device_id_type=MESH)
    pl.semaphore_wait(barrier, 3)
    for copy in firsts:
        copy.wait()

    pieces = 2
    part_rows = rows // pieces

    def views(block):
        out = [kvg.at[pl.ds(block * kv_pages, kv_pages)], pg.at[block]]
        for i in range(pieces):
            out.append(xg.at[block, pl.ds(i * part_rows, part_rows)])
        return out

    def remote(ref, send, recv, device):
        return pltpu.make_async_remote_copy(
            src_ref=ref,
            dst_ref=ref,
            send_sem=send,
            recv_sem=recv,
            device_id={"tok": device},
            device_id_type=MESH,
        )

    def forward(step, wait, send):
        for i, ref in enumerate(views(mine_at(step))):
            if wait:
                remote(ref, ring_send.at[step, i], ring_recv.at[step, i], after).wait_recv()
            if send:
                remote(ref, ring_send.at[step, i], ring_recv.at[step + 1, i], after).start()
            remote(ref, pair_send.at[step, i], pair_recv.at[step, i], partner).start()

    def take_pair(step):
        for i, ref in enumerate(views(other_at(step))):
            remote(ref, pair_send.at[step, i], pair_recv.at[step, i], partner).wait_recv()

    first_expert = tok // GROUP * group_experts

    def up(step):
        mine, other = mine_at(step), other_at(step)
        a = jnp.where(core == 0, mine, other)
        b = jnp.where(core == 0, other, mine)
        x = jnp.concatenate([xg[a], xg[b]], axis=0)
        scales = pg[a] + pg[b]
        experts_at = lax.broadcasted_iota(jnp.int32, scales.shape, 0)

        @pl.loop(0, group_experts)
        def _(l):
            pre = lax.dot_general(wbuf[l], x, TRANSPOSED, preferred_element_type=jnp.float32)
            gate, upper = pre[:units], pre[units:]
            scale = jnp.sum(
                jnp.where(experts_at == first_expert + l, scales, 0.0), axis=0, keepdims=True
            )
            act = (gate / (1.0 + jnp.exp(-gate)) * upper * scale).astype(jnp.bfloat16)
            hid[step, pl.ds(pl.multiple_of(l * units, units), units)] = act

    forward(0, False, True)

    query_rows = q_ref.shape[0]
    window = mask.shape[0]
    base = jnp.maximum(tok * query_rows + query_rows - window, 0)
    query_pos = tok * query_rows + lax.broadcasted_iota(jnp.int32, (1, query_rows), 1)
    first_pos = jnp.zeros_like(query_pos)
    end = jnp.int32(0)
    for i in range(lengths_ref.shape[0]):
        end = end + lengths_ref[i]
        first_pos = jnp.where(query_pos >= end, end, first_pos)
    key_pos = base + lax.broadcasted_iota(jnp.int32, (window, 1), 0)
    mask[...] = jnp.where((key_pos >= first_pos) & (key_pos <= query_pos), 0.0, -1e30)
    forward(1, True, True)
    take_pair(0)
    for copy in loads:
        copy.wait()
    up(0)

    @pl.loop(2, chips - 1)
    def _(step):
        forward(step, True, True)
        take_pair(step - 1)
        up(step - 1)

    def px_copy(step):
        return pltpu.make_async_remote_copy(
            src_ref=pstage.at[step],
            dst_ref=px.at[step],
            send_sem=px_send.at[step],
            recv_sem=px_recv.at[step],
            device_id={"tok": partner},
            device_id_type=MESH,
        )

    halves = 2
    cut = width // halves

    def rr_copy(step, half):
        at = pl.ds(half * cut, cut)
        return pltpu.make_async_remote_copy(
            src_ref=rstage.at[step, :, at],
            dst_ref=rr.at[step, :, at],
            send_sem=rr_send.at[step, half],
            recv_sem=rr_recv.at[step, half],
            device_id={"tok": after},
            device_id_type=MESH,
        )

    tile = 512 if width % 512 == 0 else 128

    def down(step):
        h = jnp.transpose(hid[lax.rem(step + 1, chips)])
        slot = lax.rem(step, 2)

        @pl.loop(0, width // tile)
        def _(n):
            at = pl.ds(pl.multiple_of(n * tile, tile), tile)
            part = jnp.dot(h, vbuf[:, at], preferred_element_type=jnp.float32)
            first, second = part[:rows], part[rows:]
            own[slot, :, at] = jnp.where(core == 0, first, second)
            pstage[step, :, at] = jnp.where(core == 0, second, first).astype(jnp.bfloat16)

        px_copy(step).start()

    heads = q_ref.shape[1] // head_dim
    together = 2 if heads % 2 == 0 else 1
    bundles = heads // together
    log_scale = LOG2E / math.sqrt(head_dim)

    def attend(bundle):
        at = [
            pl.ds(pl.multiple_of((bundle * together + i) * head_dim, head_dim), head_dim)
            for i in range(together)
        ]
        q = jnp.concatenate([q_ref[:, a] for a in at], axis=0)
        scores = lax.dot_general(
            keys[...], q, TRANSPOSED, preferred_element_type=jnp.float32
        )
        hide = mask[...]
        scores = scores * log_scale + jnp.concatenate([hide] * together, axis=1)
        top = jnp.max(scores, axis=0, keepdims=True)
        weights = jnp.exp2(scores - top)
        total = jnp.sum(weights, axis=0, keepdims=True)
        summed = jnp.dot(vals[...], weights.astype(jnp.bfloat16), preferred_element_type=jnp.float32)
        result = jnp.transpose(summed / total).astype(jnp.bfloat16)
        for i, a in enumerate(at):
            att_ref[:, a] = result[i * query_rows : (i + 1) * query_rows]

    def pass_on(step, receive, last):
        px_copy(step).wait_recv()
        slot = lax.rem(step, 2)
        for half in range(halves):
            at = pl.ds(half * cut, cut)
            value = own[slot, :, at] + px[step, :, at].astype(jnp.float32)
            if receive:
                rr_copy(step - 1, half).wait_recv()
                value = value + rr[step - 1, :, at].astype(jnp.float32)
            if last:
                moe_ref[:, at] = value.astype(jnp.bfloat16)
            else:
                rstage[step, :, at] = value.astype(jnp.bfloat16)
                rr_copy(step, half).start()

    down(0)
    forward(chips - 1, True, False)
    pass_on(0, False, False)
    down(1)
    take_pair(chips - 2)
    up(chips - 2)
    pass_on(1, True, False)
    down(2)
    take_pair(chips - 1)
    up(chips - 1)

    @pl.loop(0, window // page_rows)
    def _(i):
        page = table_ref[base // page_rows + i]
        block = kvg[page]
        at = pl.ds(pl.multiple_of(i * page_rows, page_rows), page_rows)
        keys[at, :] = block[:, :head_dim]
        rows_of_values[at, :] = block[:, head_dim:]

    vals[...] = jnp.transpose(rows_of_values[...])
    spans = chips - 3

    @pl.loop(2, chips - 1)
    def _(step):
        pass_on(step, True, False)
        down(step + 1)

        @pl.loop((step - 2) * bundles // spans, (step - 1) * bundles // spans)
        def _(bundle):
            attend(bundle)

    pass_on(chips - 1, True, True)

    @pl.loop(0, chips)
    def _(step):
        px_copy(step).wait_send()

    @pl.loop(0, chips - 1)
    def _(step):
        for half in range(halves):
            rr_copy(step, half).wait_send()

    @pl.loop(0, chips)
    def _(step):
        for i, ref in enumerate(views(mine_at(step))):
            remote(ref, pair_send.at[step, i], pair_recv.at[step, i], partner).wait_send()

    @pl.loop(0, chips - 1)
    def _(step):
        for i, ref in enumerate(views(mine_at(step))):
            remote(ref, ring_send.at[step, i], ring_recv.at[step, i], after).wait_send()


def ring_body(queries, kv_pool, block_table, lengths, tokens_ffn, routes, route_probs, w_in, w_out):
    devices_tok = lax.axis_size("tok")
    chips = devices_tok // 2
    _, page_rows, kv_width = kv_pool.shape
    head_dim = kv_width // 2
    pages_all = block_table.shape[0]
    keys_all = pages_all * page_rows
    query_rows = queries.shape[0]
    group_experts, units = w_in.shape[1], w_in.shape[4]
    experts = group_experts * (devices_tok // GROUP)
    rows, width = tokens_ffn.shape

    expert_rows = -(-experts // 8) * 8
    window = min(keys_all, keys_all // 2 + query_rows)
    gate_up = jnp.transpose(w_in[0], (0, 2, 3, 1))
    any_spec = pl.BlockSpec(memory_space=pl.ANY)
    vmem = pl.BlockSpec(memory_space=pltpu.VMEM)
    smem = pl.BlockSpec(memory_space=pltpu.SMEM)
    dma = pltpu.SemaphoreType.DMA
    bf16 = jnp.bfloat16
    kernel = functools.partial(fused_kernel, chips, group_experts, units, head_dim, page_rows)
    return pl.pallas_call(
        kernel,
        out_shape=(
            jax.ShapeDtypeStruct(queries.shape, bf16),
            jax.ShapeDtypeStruct(tokens_ffn.shape, bf16),
        ),
        in_specs=[any_spec, any_spec, vmem, vmem, smem, smem, vmem, any_spec, any_spec],
        out_specs=(vmem, vmem),
        scratch_shapes=[
            pltpu.VMEM((devices_tok, rows, width), bf16),
            pltpu.VMEM((pages_all, page_rows, kv_width), bf16),
            pltpu.VMEM((devices_tok, expert_rows, 2 * rows), jnp.float32),
            pltpu.VMEM((group_experts, 2 * units, width), bf16),
            pltpu.VMEM((group_experts * units, width), bf16),
            pltpu.VMEM((chips, group_experts * units, 2 * rows), bf16),
            pltpu.VMEM((window, query_rows), jnp.float32),
            pltpu.VMEM((window, head_dim), bf16),
            pltpu.VMEM((window, head_dim), bf16),
            pltpu.VMEM((head_dim, window), bf16),
            pltpu.VMEM((2, rows, width), jnp.float32),
            pltpu.VMEM((chips, rows, width), bf16),
            pltpu.VMEM((chips - 1, rows, width), bf16),
            pltpu.VMEM((chips, rows, width), bf16),
            pltpu.VMEM((chips - 1, rows, width), bf16),
            dma((2,)),
            dma((group_experts * 3,)),
            dma((chips, 4)),
            dma((chips, 4)),
            dma((chips, 4)),
            dma((chips, 4)),
            dma((chips,)),
            dma((chips,)),
            dma((chips - 1, 2)),
            dma((chips - 1, 2)),
        ],
        compiler_params=pltpu.CompilerParams(
            collective_id=0, has_side_effects=True, vmem_limit_bytes=60 * 1024 * 1024
        ),
    )(
        tokens_ffn,
        kv_pool,
        routes.T,
        route_probs.T,
        block_table,
        lengths,
        queries,
        gate_up,
        w_out[0],
    )


def solution(mesh):
    ring = mesh.shape["sec"] == 1 and mesh.shape["tok"] % 8 == 0
    chosen = ring_body if ring else body

    in_specs = (
        P(("replica", "tok"), "sec"),
        P(("replica", "tok"), None, None),
        P("replica"),
        P("replica"),
        P(("replica", "tok"), "sec"),
        P(("replica", "tok"), None),
        P(("replica", "tok"), None),
        P("tok", None, "sec", None, None),
        P("tok", None, None, "sec"),
    )
    out_specs = (P(("replica", "tok"), "sec"), P(("replica", "tok"), "sec"))
    return jax.shard_map(chosen, mesh=mesh, in_specs=in_specs, out_specs=out_specs, check_vma=False)
```
